32 devices in a mesh: grp: 2 (over y), ctx: 4 (over z), head: 2 (over x), sub: 2 (over core).
Axes of the slice: x: 2, y: 2, z: 4, core: 2. Of those that a mesh axis runs over, the one named last changes fastest.
Arguments:
- hidden: bfloat16 [8192, 4096], P(('grp', 'ctx', 'sub')), parts along dimension 0, may hold values from -6 to 6
- query_hidden: bfloat16 [512, 4096], P(('grp', 'ctx', 'sub')), parts along dimension 0, may hold values from -6 to 6
- norm_gain: float32 [4096], replicated, may hold values from 0.1 to 1.9
- w_query: bfloat16 [4096, 2048], P(None, 'head'), may hold values from -8 to 8
- w_key: bfloat16 [4096, 512], P(None, 'head'), may hold values from -1 to 1
- w_value: bfloat16 [4096, 512], P(None, 'head'), may hold values from -0.09375 to 0.09375
Outputs:
- context_out: bfloat16 [8192, 2048], P(('grp', 'ctx', 'sub'), 'head'), parts along dimension 0
- query_out: bfloat16 [512, 2048], P(('grp', 'ctx', 'sub'), 'head'), parts along dimension 0
The draws below stay inside these ranges and needn't reach their ends.
There are 2 independent parts, one for each index of `grp`. The reference program is written for one: setup_inputs(seed, part) draws one part's arguments, and reference() takes and returns one part's arrays. A program takes and returns all parts, laid end to end along the dimension named above; an argument that names none is the same for every part. Nothing has to cross between parts.
All inputs are finite; a program needn't handle non-finite values.
Results may differ from the reference program's by a relative error of at most 0.018.
The reference program's roundings to bfloat16 on the way count: a program that leaves them out, or rounds other values in their place, can miss the bound.
Values may be sent and summed in bfloat16 or wider, within the bound.
A program may use at most 128 MiB of HBM per device.

```python
import jax
import jax.numpy as jnp
from jax import lax

D = 4096
HEADS = 16
KV_HEADS = 4
HDIM = 128
CTX_DEV = 1024
Q_TOK = 256
CONTEXT = 4096
N_CTX = 4


def key_matrix(key):
    sample = jax.random.normal(jax.random.fold_in(key, 11), (D, KV_HEADS * HDIM), jnp.float32)
    return jnp.clip(sample, -6.0, 6.0) * D ** (-0.5)


def draw_w_key(key, part):
    return jnp.clip(key_matrix(key), -1.0, 1.0).astype(jnp.bfloat16)


def draw_w_query(key, part):
    noise_part = jnp.clip(jax.random.normal(jax.random.fold_in(key, 12), (D, HEADS * HDIM), jnp.float32), -6.0, 6.0) * D ** (-0.5)
    noise_part = 16.0 * noise_part
    return jnp.clip(noise_part, -8.0, 8.0).astype(jnp.bfloat16)


def shard_levels(own_key, extent, split, least, high):
    factor_of = 1.0
    for position, blocks in split:
        steps = jax.random.uniform(jax.random.fold_in(jax.random.fold_in(own_key, 6), position), (blocks,), jnp.float32, least / len(split), high / len(split))
        factor_of = factor_of * jnp.repeat(jnp.exp(steps), extent[position] // blocks).reshape((-1,) + (1,) * (len(extent) - 1 - position))
    return factor_of


def noise(stream_key, extent, width, bound, pieces=(), kind=jnp.bfloat16):
    loudness = shard_levels(stream_key, extent, pieces, -0.22, 0.18) if pieces else 1.0
    drawn = jax.random.normal(stream_key, extent, jnp.float32) * width * loudness
    return jnp.minimum(jnp.maximum(drawn, -bound), bound).astype(kind)


def setup_inputs(seed: int = 0, part: int = 0) -> dict:
    key_list = jax.random.split(jax.random.key(seed), 7)
    own_keys = jax.random.split(jax.random.fold_in(key_list[6], part), 7)
    return {
        "hidden": noise(own_keys[0], (CONTEXT, D), 1.0, 6.0, ((0, 8),)),
        "query_hidden": noise(own_keys[1], (Q_TOK, D), 1.0, 6.0, ((0, 8),)),
        "norm_gain": jnp.clip(1.0 + 0.18 * jax.random.normal(key_list[2], (D,), jnp.float32), 0.1, 1.9),
        "w_query": draw_w_query(jax.random.fold_in(key_list[6], 71), part),
        "w_key": draw_w_key(jax.random.fold_in(key_list[6], 71), part),
        "w_value": noise(key_list[5], (D, KV_HEADS * HDIM), D ** -0.5, 0.09375, ((1, 2),)),
    }


rope_base = 500000.0
norm_eps = 1e-05
masked_score = -1e+30

def normalize(states, norm_gain):
    widened = states.astype(jnp.float32)
    meansq = lax.optimization_barrier(jnp.mean(widened * widened, axis=-1, keepdims=True)) + norm_eps
    return (widened * lax.rsqrt(meansq) * norm_gain).astype(jnp.bfloat16)

def rotate(tensor, positions):
    half_dim = tensor.shape[-1] // 2
    inverse = rope_base ** (-(jnp.arange(half_dim, dtype=jnp.float32) * 2.0 / tensor.shape[-1]))
    angles = positions.astype(jnp.float32)[:, None] * inverse[None, :]
    cosine = jnp.cos(angles)[:, None, :]
    sine_part = jnp.sin(angles)[:, None, :]
    lower_half = tensor[..., :half_dim]
    upper_half = tensor[..., half_dim:]
    return jnp.concatenate([lower_half * cosine - upper_half * sine_part, upper_half * cosine + lower_half * sine_part], axis=-1)

def project(normed, positions, w_query, w_key, w_value):
    row_count = normed.shape[0]
    query_heads = jnp.dot(normed, w_query, preferred_element_type=jnp.float32).reshape(row_count, -1, HDIM)
    key_heads = jnp.dot(normed, w_key, preferred_element_type=jnp.float32).reshape(row_count, -1, HDIM)
    value_heads = jnp.dot(normed, w_value, preferred_element_type=jnp.float32).reshape(row_count, -1, HDIM)
    return (rotate(query_heads, positions).astype(jnp.bfloat16), rotate(key_heads, positions).astype(jnp.bfloat16), value_heads.astype(jnp.bfloat16))

def attend(query_heads, key_heads, value_heads, visible):
    row_count = query_heads.shape[0]
    head_count = query_heads.shape[1]
    kv_count = key_heads.shape[1]
    grouped = query_heads.reshape(row_count, kv_count, head_count // kv_count, HDIM)
    scores = jnp.einsum('nkgd,mkd->nkgm', grouped.astype(jnp.float32), key_heads.astype(jnp.float32)) * HDIM ** (-0.5)
    mask_full = visible[:, None, None, :]
    scores = jnp.where(mask_full, scores, masked_score)
    maxima = lax.optimization_barrier(jnp.max(scores, axis=-1))
    weights = jnp.where(mask_full, jnp.exp(scores - maxima[..., None]), 0.0)
    totals = lax.optimization_barrier(jnp.sum(weights, axis=-1))
    rounded = lax.optimization_barrier(weights.astype(jnp.bfloat16)).astype(jnp.float32)
    accumulated = jnp.einsum('nkgm,mkd->nkgd', rounded, value_heads.astype(jnp.float32))
    return (maxima.reshape(row_count, head_count), totals.reshape(row_count, head_count), accumulated.reshape(row_count, head_count, HDIM))

def reference(hidden, query_hidden, norm_gain, w_query, w_key, w_value):
    context_len = CTX_DEV * N_CTX
    positions = jnp.arange(context_len, dtype=jnp.int32)
    queries, key_rows, value_rows = project(normalize(hidden, norm_gain), positions, w_query, w_key, w_value)
    query_positions = context_len + jnp.arange(Q_TOK, dtype=jnp.int32)
    query_heads, query_keys, query_values = project(normalize(query_hidden, norm_gain), query_positions, w_query, w_key, w_value)
    anchor_keys = key_rows[:CTX_DEV]
    anchor_values = value_rows[:CTX_DEV]
    offsets = jnp.arange(CTX_DEV, dtype=jnp.int32)
    causal = offsets[:, None] >= offsets[None, :]

    def one_block(blocked):
        block_q, block_k, block_v, block_index = blocked
        all_keys = jnp.concatenate([anchor_keys, block_k], axis=0)
        all_values = jnp.concatenate([anchor_values, block_v], axis=0)
        visible = jnp.concatenate([jnp.broadcast_to(block_index > 0, (CTX_DEV, CTX_DEV)), causal], axis=1)
        maxima, totals, accumulated = attend(block_q, all_keys, all_values, visible)
        return (accumulated / totals[..., None]).astype(jnp.bfloat16).reshape(CTX_DEV, HEADS * HDIM)
    context_out = lax.map(one_block, (queries.reshape(N_CTX, CTX_DEV, HEADS, HDIM), key_rows.reshape(N_CTX, CTX_DEV, KV_HEADS, HDIM), value_rows.reshape(N_CTX, CTX_DEV, KV_HEADS, HDIM), jnp.arange(N_CTX, dtype=jnp.int32))).reshape(context_len, HEADS * HDIM)
    every_key = jnp.concatenate([key_rows, query_keys], axis=0)
    every_value = jnp.concatenate([value_rows, query_values], axis=0)
    block_rows = Q_TOK // N_CTX

    def one_rows(blocked):
        rows_q, rows_pos = blocked
        visible = jnp.concatenate([jnp.ones((block_rows, context_len), dtype=bool), rows_pos[:, None] >= query_positions[None, :]], axis=1)
        maxima, totals, accumulated = attend(rows_q, every_key, every_value, visible)
        return (accumulated / totals[..., None]).astype(jnp.bfloat16).reshape(block_rows, HEADS * HDIM)
    query_out = lax.map(one_rows, (query_heads.reshape(N_CTX, block_rows, HEADS, HDIM), query_positions.reshape(N_CTX, block_rows))).reshape(Q_TOK, HEADS * HDIM)
    return (context_out, query_out)
```

```python
import functools
import math

import jax
import jax.numpy as jnp
from jax import lax
from jax.experimental import pallas as pl
from jax.experimental.pallas import tpu as pltpu
from jax.sharding import PartitionSpec as P

HDIM = 128
TILE = 128
CHUNKS = 4

rope_base = 500000.0
norm_eps = 1e-05
masked_score = -1e30
exponent_scale = HDIM ** (-0.5) * math.log2(math.e)

MESH = pl.DeviceIdType.MESH
NT_DIMS = (((1,), (1,)), ((), ()))


def kernel(
    sizes,
    hidden_hbm, qhidden_hbm, gain_ref, cos_ref, sin_ref, wq_hbm, wk_hbm, wv_hbm,
    out_ref, qout_ref,
    hid, qhid, normed, wq, wk, wv, heads_q, own_q, all_q, blk, qkv, anc,
    acc1, max1, sacc, sstat, racc, rstat,
    load_sem, qload_sem, wk_sem, wv_sem, wq_sem,
    blk_sem, qkv_sem, chain_send, chain_recv, pair_send, pair_recv,
    q_send, q_recv, r_send, r_recv, t_send, t_recv,
):
    ctx_count, sub_count, query_rows = sizes
    rows, width = hid.shape
    padded = qhid.shape[0]
    q_heads = heads_q.shape[0]
    key_cols = wk.shape[1]
    kv_heads = key_cols // HDIM
    group = q_heads // kv_heads
    tiles = rows // TILE
    part = rows // CHUNKS
    ctx = lax.axis_index("ctx")
    sub = lax.axis_index("sub")
    peer = lax.rem(sub + 1, sub_count)

    def load_rows(i):
        piece = pl.ds(i * TILE, TILE)
        return pltpu.make_async_copy(hidden_hbm.at[piece], hid.at[piece], load_sem.at[i])

    wq_width = wq.shape[2]
    wq_tiles = wq.shape[0]

    def load_wq(j):
        return pltpu.make_async_copy(
            wq_hbm.at[:, pl.ds(j * wq_width, wq_width)], wq.at[j], wq_sem.at[j]
        )

    load_query = pltpu.make_async_copy(qhidden_hbm, qhid, qload_sem)
    load_wk = pltpu.make_async_copy(wk_hbm, wk, wk_sem)
    load_wv = pltpu.make_async_copy(wv_hbm, wv, wv_sem)
    for i in range(tiles):
        load_rows(i).start()
    load_query.start()
    load_wk.start()
    load_wv.start()
    for j in range(wq_tiles):
        load_wq(j).start()

    barrier = pltpu.get_barrier_semaphore()
    for step in range(1, ctx_count):
        other = lax.rem(ctx + step, ctx_count)
        pl.semaphore_signal(barrier, inc=1, device_id={"ctx": other}, device_id_type=MESH)
    pl.semaphore_signal(barrier, inc=1, device_id={"sub": peer}, device_id_type=MESH)

    gain = gain_ref[...]

    def norm_rows(source, start, target, count):
        wide = source[pl.ds(start, count), :].astype(jnp.float32)
        meansq = jnp.mean(wide * wide, axis=-1, keepdims=True) + norm_eps
        normed[pl.ds(target, count), :] = (wide * lax.rsqrt(meansq) * gain).astype(jnp.bfloat16)

    for i in range(tiles):
        load_rows(i).wait()

        @pl.loop(0, TILE // 16)
        def _(b):
            start = pl.multiple_of(i * TILE + b * 16, 16)
            norm_rows(hid, start, start, 16)

    load_query.wait()
    for b in range(padded // 16):
        norm_rows(qhid, b * 16, rows + b * 16, 16)

    def rotated(values, head):
        cols = values[:, head * HDIM:(head + 1) * HDIM]
        return (cols * cos_ref[...] + pltpu.roll(cols, HDIM // 2, 1) * sin_ref[...]).astype(
            jnp.bfloat16
        )

    load_wk.wait()
    keys = jnp.dot(normed[...], wk[...], preferred_element_type=jnp.float32)
    for h in range(kv_heads):
        turned = rotated(keys, h)
        blk[sub, :, pl.ds(h * HDIM, HDIM)] = turned[:rows]
        qkv[sub, :, pl.ds(h * HDIM, HDIM)] = turned[rows:]
    load_wv.wait()
    values = jnp.dot(normed[...], wv[...], preferred_element_type=jnp.float32).astype(jnp.bfloat16)
    blk[sub, :, pl.ds(key_cols, key_cols)] = values[:rows]
    qkv[sub, :, pl.ds(key_cols, key_cols)] = values[rows:]

    pl.semaphore_wait(barrier, ctx_count)

    below = lax.rem(ctx + 1, ctx_count)

    def send_first(i):
        return pltpu.make_async_remote_copy(
            blk.at[sub, pl.ds(i * part, part)], anc.at[sub, i],
            chain_send.at[i], chain_recv.at[i],
            device_id={"ctx": below}, device_id_type=MESH,
        )

    def send_on(i):
        return pltpu.make_async_remote_copy(
            anc.at[sub, i], anc.at[sub, i],
            chain_send.at[i], chain_recv.at[i],
            device_id={"ctx": below}, device_id_type=MESH,
        )

    def send_pair(i):
        return pltpu.make_async_remote_copy(
            anc.at[sub, i], anc.at[sub, i],
            pair_send.at[i], pair_recv.at[i],
            device_id={"sub": peer}, device_id_type=MESH,
        )

    def recv_pair(i):
        return pltpu.make_async_remote_copy(
            anc.at[peer, i], anc.at[peer, i],
            pair_send.at[i], pair_recv.at[i],
            device_id={"sub": peer}, device_id_type=MESH,
        )

    @pl.when(ctx == 0)
    def _():
        for i in range(CHUNKS):
            send_first(i).start()

    def swap(ref, sems, place):
        return pltpu.make_async_remote_copy(
            ref.at[place], ref.at[place], sems.at[0], sems.at[1],
            device_id={"sub": peer}, device_id_type=MESH,
        )

    swap(blk, blk_sem, sub).start()
    swap(qkv, qkv_sem, sub).start()

    def forward(i, which):
        @pl.when(which)
        def _():
            send_on(i).wait_recv()

            @pl.when(ctx < ctx_count - 1)
            def _():
                send_on(i).start()

            send_pair(i).start()

    per_tile = wq_width // HDIM
    for j in range(wq_tiles):
        load_wq(j).wait()

        made = jnp.dot(normed[...], wq[j], preferred_element_type=jnp.float32)
        for t in range(per_tile):
            turned = rotated(made, t)
            heads_q[j * per_tile + t] = turned[:rows]
            own_q[j * per_tile + t] = turned[rows:]

    def send_query(step):
        other = lax.rem(ctx + step, ctx_count)
        return pltpu.make_async_remote_copy(
            own_q, all_q.at[ctx], q_send.at[other], q_recv.at[ctx],
            device_id={"ctx": other}, device_id_type=MESH,
        )

    def recv_query(step):
        other = lax.rem(ctx + step, ctx_count)
        return pltpu.make_async_remote_copy(
            own_q, all_q.at[other], q_send.at[other], q_recv.at[other],
            device_id={"ctx": other}, device_id_type=MESH,
        )

    for step in range(1, ctx_count):
        send_query(step).start()
    all_q[ctx] = own_q[...]

    forward(0, ctx == 1)

    def scores_of(q, k):
        return lax.dot_general(q, k, NT_DIMS, preferred_element_type=jnp.float32)

    def weights_of(s, m):
        return jnp.exp2((s - m) * exponent_scale).astype(jnp.bfloat16)

    def with_ones(v):
        return jnp.concatenate([v, jnp.ones_like(v)], axis=1)

    def add_up(p, v):
        return jnp.dot(p, with_ones(v), preferred_element_type=jnp.float32)

    def kcols(kh):
        return slice(kh * HDIM, (kh + 1) * HDIM)

    def vcols(kh):
        return slice(key_cols + kh * HDIM, key_cols + (kh + 1) * HDIM)

    def tile_q(kh, start):
        return heads_q[kh * group:(kh + 1) * group, pl.ds(start, TILE), :].reshape(
            group * TILE, HDIM
        )

    for t in range(tiles):
        span = (t + 1) * TILE
        for kh in range(kv_heads):
            s = scores_of(tile_q(kh, t * TILE), blk[sub, :span, kcols(kh)])
            row = lax.broadcasted_iota(jnp.int32, (TILE, span), 0) + t * TILE
            col = lax.broadcasted_iota(jnp.int32, (TILE, span), 1)
            s = jnp.where(
                (row >= col)[None], s.reshape(group, TILE, span), masked_score
            ).reshape(group * TILE, span)
            m = jnp.max(s, axis=-1, keepdims=True)
            acc1[kh, t] = add_up(weights_of(s, m), blk[sub, :span, vcols(kh)])
            max1[kh, t] = jnp.broadcast_to(m, (group * TILE, HDIM))
        if t == tiles // 2 - 1:
            forward(1, ctx == 1)

    forward(2, ctx == 1)
    forward(0, ctx == 2)

    def merged(kh, t, k, v):
        s = scores_of(tile_q(kh, pl.multiple_of(t * TILE, TILE)), k)
        before = max1[kh, t]
        m = jnp.maximum(jnp.max(s, axis=-1, keepdims=True), before)
        factor = jnp.exp2((before - m) * exponent_scale)
        acc = acc1[kh, t] * jnp.concatenate([factor, factor], axis=1)
        return m, acc + add_up(weights_of(s, m[:, :1]), v)

    swap(blk, blk_sem, peer).wait_recv()
    swap(qkv, qkv_sem, peer).wait_recv()

    @pl.when(sub > 0)
    def _():
        @pl.loop(0, tiles)
        def _(t):
            for kh in range(kv_heads):
                m, acc = merged(kh, t, blk[0, :, kcols(kh)], blk[0, :, vcols(kh)])
                acc1[kh, t] = acc
                max1[kh, t] = m

    forward(3, ctx == 1)
    forward(1, ctx == 2)

    for step in range(1, ctx_count):
        recv_query(step).wait_recv()

    total = ctx_count * group * padded
    keys_q = sub_count * padded
    shape4 = (ctx_count, group, padded, keys_q)
    owner = lax.broadcasted_iota(jnp.int32, shape4, 0)
    place = lax.broadcasted_iota(jnp.int32, shape4, 2)
    key_at = lax.broadcasted_iota(jnp.int32, shape4, 3)
    query_pos = (owner * sub_count + sub) * query_rows + place
    key_sub = jnp.where(key_at >= padded, 1, 0)
    key_row = key_at - key_sub * padded
    key_pos = (ctx * sub_count + key_sub) * query_rows + key_row
    seen = (query_pos >= key_pos) & (key_row < query_rows)
    lane = lax.broadcasted_iota(jnp.int32, (padded, HDIM), 1)
    stats = [jnp.zeros((padded, HDIM), jnp.float32) for _ in range(ctx_count)]
    for kh in range(kv_heads):
        span = slice(kh * group, (kh + 1) * group)
        q = all_q[:, span].reshape(total, HDIM)
        block = blk[:, :, kcols(kh)].reshape(sub_count * rows, HDIM)
        near = qkv[:, :, kcols(kh)].reshape(keys_q, HDIM)
        s0 = scores_of(q, block)
        s1 = jnp.where(
            seen, scores_of(q, near).reshape(shape4), masked_score
        ).reshape(total, keys_q)
        m = jnp.maximum(
            jnp.max(s0, axis=-1, keepdims=True), jnp.max(s1, axis=-1, keepdims=True)
        )
        acc = add_up(
            weights_of(s0, m), blk[:, :, vcols(kh)].reshape(sub_count * rows, HDIM)
        ) + add_up(weights_of(s1, m), qkv[:, :, vcols(kh)].reshape(keys_q, HDIM))
        sacc[:, span] = acc[:, :HDIM].astype(jnp.bfloat16).reshape(
            ctx_count, group, padded, HDIM
        )
        sums = acc[:, HDIM:]
        for z in range(ctx_count):
            for g in range(group):
                cut = slice((z * group + g) * padded, (z * group + g + 1) * padded)
                head = kh * group + g
                stats[z] = jnp.where(lane == head, m[cut], stats[z])
                stats[z] = jnp.where(lane == HDIM // 2 + head, sums[cut], stats[z])
    for z in range(ctx_count):
        sstat[z] = stats[z]

    def send_result(step, other, home):
        return pltpu.make_async_remote_copy(
            sacc.at[other], racc.at[home], r_send.at[other], r_recv.at[home],
            device_id={"ctx": other}, device_id_type=MESH,
        )

    def send_stat(step, other, home):
        return pltpu.make_async_remote_copy(
            sstat.at[other], rstat.at[home], t_send.at[other], t_recv.at[home],
            device_id={"ctx": other}, device_id_type=MESH,
        )

    for step in range(1, ctx_count):
        other = lax.rem(ctx + step, ctx_count)
        send_result(step, other, ctx).start()
        send_stat(step, other, ctx).start()
    racc[ctx] = sacc[ctx]
    rstat[ctx] = sstat[ctx]

    forward(2, ctx == 2)
    forward(3, ctx == 2)
    for i in range(CHUNKS):
        forward(i, ctx > 2)

    def finish(kh, t, acc):
        done = (acc[:, :HDIM] / acc[:, HDIM:]).astype(jnp.bfloat16)
        start = pl.multiple_of(t * TILE, TILE)
        for g in range(group):
            head = kh * group + g
            out_ref[pl.ds(start, TILE), head * HDIM:(head + 1) * HDIM] = done[
                g * TILE:(g + 1) * TILE
            ]

    @pl.when(ctx == 0)
    def _():
        @pl.loop(0, tiles)
        def _(t):
            for kh in range(kv_heads):
                finish(kh, t, acc1[kh, t])

    @pl.when(ctx > 0)
    def _():
        for i in range(CHUNKS):
            recv_pair(i).wait_recv()

        @pl.loop(0, tiles)
        def _(t):
            for kh in range(kv_heads):
                _, acc = merged(
                    kh, t,
                    anc[:, :, :, kcols(kh)].reshape(sub_count * rows, HDIM),
                    anc[:, :, :, vcols(kh)].reshape(sub_count * rows, HDIM),
                )
                finish(kh, t, acc)

    for step in range(1, ctx_count):
        other = lax.rem(ctx + step, ctx_count)
        send_result(step, ctx, other).wait_recv()
        send_stat(step, ctx, other).wait_recv()

    got = [rstat[z] for z in range(ctx_count)]
    top = functools.reduce(jnp.maximum, got)
    scaled = [jnp.exp2((one - top) * exponent_scale) for one in got]
    for h in range(q_heads):
        above = jnp.zeros((padded, HDIM), jnp.float32)
        under = jnp.zeros((padded, 1), jnp.float32)
        for z in range(ctx_count):
            w = scaled[z][:, h:h + 1]
            above = above + w * racc[z, h].astype(jnp.float32)
            under = under + w * got[z][:, HDIM // 2 + h:HDIM // 2 + h + 1]
        qout_ref[:, h * HDIM:(h + 1) * HDIM] = (above / under).astype(jnp.bfloat16)

    swap(blk, blk_sem, sub).wait_send()
    swap(qkv, qkv_sem, sub).wait_send()
    for step in range(1, ctx_count):
        other = lax.rem(ctx + step, ctx_count)
        send_query(step).wait_send()
        send_result(step, other, ctx).wait_send()
        send_stat(step, other, ctx).wait_send()

    @pl.when(ctx == 0)
    def _():
        for i in range(CHUNKS):
            send_first(i).wait_send()

    @pl.when(ctx > 0)
    def _():
        for i in range(CHUNKS):
            send_pair(i).wait_send()

    @pl.when((ctx > 0) & (ctx < ctx_count - 1))
    def _():
        for i in range(CHUNKS):
            send_on(i).wait_send()


def turns(positions):
    half = HDIM // 2
    inverse = rope_base ** (-(jnp.arange(half, dtype=jnp.float32) * 2.0 / HDIM))
    angles = positions.astype(jnp.float32)[:, None] * inverse[None, :]
    cosine = jnp.cos(angles)
    sine = jnp.sin(angles)
    return (
        jnp.concatenate([cosine, cosine], axis=1),
        jnp.concatenate([-sine, sine], axis=1),
    )


def shards(hidden, query_hidden, norm_gain, w_query, w_key, w_value):
    rows, width = hidden.shape
    query_rows = query_hidden.shape[0]
    padded = -(-query_rows // 16) * 16
    q_cols = w_query.shape[1]
    key_cols = w_key.shape[1]
    q_heads = q_cols // HDIM
    kv_heads = key_cols // HDIM
    group = q_heads // kv_heads
    tiles = rows // TILE
    ctx_count = lax.axis_size("ctx")
    sub_count = lax.axis_size("sub")
    ctx = lax.axis_index("ctx")
    sub = lax.axis_index("sub")
    if padded != query_rows:
        query_hidden = jnp.pad(query_hidden, ((0, padded - query_rows), (0, 0)))
    slot = ctx * sub_count + sub
    positions = jnp.concatenate(
        [
            slot * rows + jnp.arange(rows, dtype=jnp.int32),
            ctx_count * sub_count * rows
            + slot * query_rows
            + jnp.arange(padded, dtype=jnp.int32),
        ]
    )
    cosine, sine = turns(positions)
    wq_width = min(256, q_cols)
    bf16, f32 = jnp.bfloat16, jnp.float32
    dma = pltpu.SemaphoreType.DMA
    vmem = pl.BlockSpec(memory_space=pltpu.VMEM)
    hbm = pl.BlockSpec(memory_space=pl.ANY)
    out, qout = pl.pallas_call(
        functools.partial(kernel, (ctx_count, sub_count, query_rows)),
        out_shape=(
            jax.ShapeDtypeStruct((rows, q_cols), bf16),
            jax.ShapeDtypeStruct((padded, q_cols), bf16),
        ),
        in_specs=[hbm, hbm, vmem, vmem, vmem, hbm, hbm, hbm],
        out_specs=(vmem, vmem),
        scratch_shapes=[
            pltpu.VMEM((rows, width), bf16),
            pltpu.VMEM((padded, width), bf16),
            pltpu.VMEM((rows + padded, width), bf16),
            pltpu.VMEM((q_cols // wq_width, width, wq_width), bf16),
            pltpu.VMEM((width, key_cols), bf16),
            pltpu.VMEM((width, key_cols), bf16),
            pltpu.VMEM((q_heads, rows, HDIM), bf16),
            pltpu.VMEM((q_heads, padded, HDIM), bf16),
            pltpu.VMEM((ctx_count, q_heads, padded, HDIM), bf16),
            pltpu.VMEM((sub_count, rows, 2 * key_cols), bf16),
            pltpu.VMEM((sub_count, padded, 2 * key_cols), bf16),
            pltpu.VMEM((sub_count, CHUNKS, rows // CHUNKS, 2 * key_cols), bf16),
            pltpu.VMEM((kv_heads, tiles, group * TILE, 2 * HDIM), f32),
            pltpu.VMEM((kv_heads, tiles, group * TILE, HDIM), f32),
            pltpu.VMEM((ctx_count, q_heads, padded, HDIM), bf16),
            pltpu.VMEM((ctx_count, padded, HDIM), f32),
            pltpu.VMEM((ctx_count, q_heads, padded, HDIM), bf16),
            pltpu.VMEM((ctx_count, padded, HDIM), f32),
            dma((tiles,)), dma, dma, dma, dma((q_cols // wq_width,)),
            dma((2,)), dma((2,)),
            dma((CHUNKS,)), dma((CHUNKS,)), dma((CHUNKS,)), dma((CHUNKS,)),
            dma((ctx_count,)), dma((ctx_count,)), dma((ctx_count,)), dma((ctx_count,)),
            dma((ctx_count,)), dma((ctx_count,)),
        ],
        compiler_params=pltpu.CompilerParams(
            collective_id=0, has_side_effects=True, vmem_limit_bytes=58 * 1024 * 1024
        ),
    )(hidden, query_hidden, norm_gain.reshape(1, width), cosine, sine, w_query, w_key, w_value)
    return out, qout[:query_rows]


def solution(mesh):
    return jax.shard_map(
        shards,
        mesh=mesh,
        in_specs=(
            P(("grp", "ctx", "sub"), None),
            P(("grp", "ctx", "sub"), None),
            P(),
            P(None, "head"),
            P(None, "head"),
            P(None, "head"),
        ),
        out_specs=(P(("grp", "ctx", "sub"), "head"), P(("grp", "ctx", "sub"), "head")),
        check_vma=False,
    )
```

```python
import functools
import math

import jax
import jax.numpy as jnp
from jax import lax
from jax.experimental import pallas as pl
from jax.experimental.pallas import tpu as pltpu
from jax.sharding import PartitionSpec as P

HDIM = 128
TILE = 128
CHUNKS = 8

LATEST = 3
SCHEDULE = {
    1: ["q1", "q2", "q3", "q3", "d1", "d3", "peer", "peer"],
    2: ["q3", "d1", "d3", "peer", "peer", "peer", "near0", "near1"],
    LATEST: ["peer", "peer", "peer", "near0", "near0", "near1", "near1", "near1"],
}

rope_base = 500000.0
norm_eps = 1e-05
masked_score = -1e30
exponent_scale = HDIM ** (-0.5) * math.log2(math.e)

MESH = pl.DeviceIdType.MESH
NT_DIMS = (((1,), (1,)), ((), ()))


def kernel(
    sizes,
    hidden_hbm, qhidden_hbm, gain_ref, cosine_ref, sine_ref, wq_hbm, wk_hbm, wv_hbm,
    out_ref, qout_ref,
    hid, qhid, normed, wq, wk, wv, heads_q, own_q, all_q, blk, qkv, anc,
    acc1, max1, sacc, sstat, racc, rstat, cos_ref, sin_ref,
    load_sem, qload_sem, wk_sem, wv_sem, wq_sem,
    blk_sem, qkv_sem, chain_send, chain_recv, pair_send, pair_recv,
    q_send, q_recv, r_send, r_recv, t_send, t_recv,
):
    ctx_count, sub_count, query_rows = sizes
    rows, width = hid.shape
    padded = qhid.shape[0]
    q_heads = heads_q.shape[0]
    key_cols = wk.shape[1]
    kv_heads = key_cols // HDIM
    group = q_heads // kv_heads
    tiles = rows // TILE
    part = rows // CHUNKS
    ctx = lax.axis_index("ctx")
    sub = lax.axis_index("sub")
    peer = lax.rem(sub + 1, sub_count)

    def load_rows(i):
        piece = pl.ds(i * TILE, TILE)
        return pltpu.make_async_copy(hidden_hbm.at[piece], hid.at[piece], load_sem.at[i])

    wq_width = wq.shape[2]
    wq_tiles = wq.shape[0]

    def load_wq(j):
        return pltpu.make_async_copy(
            wq_hbm.at[:, pl.ds(j * wq_width, wq_width)], wq.at[j], wq_sem.at[j]
        )

    load_query = pltpu.make_async_copy(qhidden_hbm, qhid, qload_sem)
    load_wk = pltpu.make_async_copy(wk_hbm, wk, wk_sem)
    load_wv = pltpu.make_async_copy(wv_hbm, wv, wv_sem)
    for i in range(tiles):
        load_rows(i).start()
    load_query.start()
    load_wk.start()
    load_wv.start()
    for j in range(wq_tiles):
        load_wq(j).start()

    barrier = pltpu.get_barrier_semaphore()
    for step in range(1, ctx_count):
        other = lax.rem(ctx + step, ctx_count)
        pl.semaphore_signal(barrier, inc=1, device_id={"ctx": other}, device_id_type=MESH)
    pl.semaphore_signal(barrier, inc=1, device_id={"sub": peer}, device_id_type=MESH)

    cos_ref[...] = jnp.concatenate([cosine_ref[...], cosine_ref[...]], axis=1)
    sin_ref[...] = jnp.concatenate([-sine_ref[...], sine_ref[...]], axis=1)
    gain = gain_ref[...]

    def norm_rows(source, start, target, count):
        wide = source[pl.ds(start, count), :].astype(jnp.float32)
        meansq = jnp.mean(wide * wide, axis=-1, keepdims=True) + norm_eps
        wide = source[pl.ds(start, count), :].astype(jnp.float32)
        normed[pl.ds(target, count), :] = (wide * lax.rsqrt(meansq) * gain).astype(jnp.bfloat16)

    for i in range(tiles):
        load_rows(i).wait()

        @pl.loop(0, TILE // 16, unroll=2)
        def _(b):
            start = pl.multiple_of(i * TILE + b * 16, 16)
            norm_rows(hid, start, start, 16)

    load_query.wait()
    for b in range(padded // 16):
        norm_rows(qhid, b * 16, rows + b * 16, 16)

    def rotated(values, head):
        cols = values[:, head * HDIM:(head + 1) * HDIM]
        return (cols * cos_ref[...] + pltpu.roll(cols, HDIM // 2, 1) * sin_ref[...]).astype(
            jnp.bfloat16
        )

    load_wk.wait()
    keys = jnp.dot(normed[...], wk[...], preferred_element_type=jnp.float32)
    for h in range(kv_heads):
        turned = rotated(keys, h)
        blk[sub, :, pl.ds(h * HDIM, HDIM)] = turned[:rows]
        qkv[sub, :, pl.ds(h * HDIM, HDIM)] = turned[rows:]
    load_wv.wait()
    values = jnp.dot(normed[...], wv[...], preferred_element_type=jnp.float32).astype(jnp.bfloat16)
    blk[sub, :, pl.ds(key_cols, key_cols)] = values[:rows]
    qkv[sub, :, pl.ds(key_cols, key_cols)] = values[rows:]

    pl.semaphore_wait(barrier, ctx_count)

    below = lax.rem(ctx + 1, ctx_count)

    def send_first(i):
        return pltpu.make_async_remote_copy(
            blk.at[sub, pl.ds(i * part, part)], anc.at[sub, i],
            chain_send.at[i], chain_recv.at[i],
            device_id={"ctx": below}, device_id_type=MESH,
        )

    def send_on(i):
        return pltpu.make_async_remote_copy(
            anc.at[sub, i], anc.at[sub, i],
            chain_send.at[i], chain_recv.at[i],
            device_id={"ctx": below}, device_id_type=MESH,
        )

    def send_pair(i):
        return pltpu.make_async_remote_copy(
            anc.at[sub, i], anc.at[sub, i],
            pair_send.at[i], pair_recv.at[i],
            device_id={"sub": peer}, device_id_type=MESH,
        )

    def recv_pair(i):
        return pltpu.make_async_remote_copy(
            anc.at[peer, i], anc.at[peer, i],
            pair_send.at[i], pair_recv.at[i],
            device_id={"sub": peer}, device_id_type=MESH,
        )

    @pl.when(ctx == 0)
    def _():
        for i in range(CHUNKS):
            send_first(i).start()

    def swap(ref, sems, place):
        return pltpu.make_async_remote_copy(
            ref.at[place], ref.at[place], sems.at[0], sems.at[1],
            device_id={"sub": peer}, device_id_type=MESH,
        )

    swap(blk, blk_sem, sub).start()
    swap(qkv, qkv_sem, sub).start()

    def forward(i):
        send_on(i).wait_recv()

        @pl.when(ctx < ctx_count - 1)
        def _():
            send_on(i).start()

        send_pair(i).start()

    def point(name):
        for place, plan in SCHEDULE.items():
            due = [i for i in range(CHUNKS) if plan[i] == name]
            if due:
                @pl.when(ctx >= place if place == LATEST else ctx == place)
                def _():
                    for i in due:
                        forward(i)

    per_tile = wq_width // HDIM
    for j in range(wq_tiles):
        load_wq(j).wait()

        made = jnp.dot(normed[...], wq[j], preferred_element_type=jnp.float32)
        for t in range(per_tile):
            turned = rotated(made, t)
            heads_q[j * per_tile + t] = turned[:rows]
            own_q[j * per_tile + t] = turned[rows:]
        for at in range(3):
            if at * wq_tiles // 4 == j:
                point(f"q{at}")

    def send_query(step):
        other = lax.rem(ctx + step, ctx_count)
        return pltpu.make_async_remote_copy(
            own_q, all_q.at[ctx], q_send.at[other], q_recv.at[ctx],
            device_id={"ctx": other}, device_id_type=MESH,
        )

    def recv_query(step):
        other = lax.rem(ctx + step, ctx_count)
        return pltpu.make_async_remote_copy(
            own_q, all_q.at[other], q_send.at[other], q_recv.at[other],
            device_id={"ctx": other}, device_id_type=MESH,
        )

    for step in range(1, ctx_count):
        send_query(step).start()
    all_q[ctx] = own_q[...]

    point("q3")

    def scores_of(q, k):
        return lax.dot_general(q, k, NT_DIMS, preferred_element_type=jnp.float32)

    def weights_of(s, m):
        return jnp.exp2((s - m) * exponent_scale).astype(jnp.bfloat16)

    def with_ones(v):
        return jnp.concatenate([v, jnp.ones_like(v)], axis=1)

    def add_up(p, v):
        return jnp.dot(p, with_ones(v), preferred_element_type=jnp.float32)

    def kcols(kh):
        return slice(kh * HDIM, (kh + 1) * HDIM)

    def vcols(kh):
        return slice(key_cols + kh * HDIM, key_cols + (kh + 1) * HDIM)

    def tile_q(kh, start):
        return heads_q[kh * group:(kh + 1) * group, pl.ds(start, TILE), :].reshape(
            group * TILE, HDIM
        )

    for t in range(tiles):
        span = (t + 1) * TILE
        for kh in range(kv_heads):
            s = scores_of(tile_q(kh, t * TILE), blk[sub, :span, kcols(kh)])
            row = lax.broadcasted_iota(jnp.int32, (TILE, span), 0) + t * TILE
            col = lax.broadcasted_iota(jnp.int32, (TILE, span), 1)
            s = jnp.where(
                (row >= col)[None], s.reshape(group, TILE, span), masked_score
            ).reshape(group * TILE, span)
            m = jnp.max(s, axis=-1, keepdims=True)
            acc1[kh, t] = add_up(weights_of(s, m), blk[sub, :span, vcols(kh)])
            max1[kh, t] = jnp.broadcast_to(m, (group * TILE, HDIM))
        for at in range(4):
            if at * tiles // 4 == t:
                point(f"d{at}")

    def merged(kh, t, k, v):
        s = scores_of(tile_q(kh, pl.multiple_of(t * TILE, TILE)), k)
        before = max1[kh, t]
        m = jnp.maximum(jnp.max(s, axis=-1, keepdims=True), before)
        factor = jnp.exp2((before - m) * exponent_scale)
        acc = acc1[kh, t] * jnp.concatenate([factor, factor], axis=1)
        return m, acc + add_up(weights_of(s, m[:, :1]), v)

    swap(blk, blk_sem, peer).wait_recv()
    swap(qkv, qkv_sem, peer).wait_recv()

    @pl.when(sub > 0)
    def _():
        @pl.loop(0, tiles)
        def _(t):
            for kh in range(kv_heads):
                m, acc = merged(kh, t, blk[0, :, kcols(kh)], blk[0, :, vcols(kh)])
                acc1[kh, t] = acc
                max1[kh, t] = m

    point("peer")

    for step in range(1, ctx_count):
        recv_query(step).wait_recv()

    total = ctx_count * group * padded
    keys_q = sub_count * padded
    shape4 = (ctx_count, group, padded, keys_q)
    owner = lax.broadcasted_iota(jnp.int32, shape4, 0)
    place = lax.broadcasted_iota(jnp.int32, shape4, 2)
    key_at = lax.broadcasted_iota(jnp.int32, shape4, 3)
    query_pos = (owner * sub_count + sub) * query_rows + place
    key_sub = jnp.where(key_at >= padded, 1, 0)
    key_row = key_at - key_sub * padded
    key_pos = (ctx * sub_count + key_sub) * query_rows + key_row
    seen = (query_pos >= key_pos) & (key_row < query_rows)
    lane = lax.broadcasted_iota(jnp.int32, (padded, HDIM), 1)
    stats = [jnp.zeros((padded, HDIM), jnp.float32) for _ in range(ctx_count)]
    for kh in range(kv_heads):
        span = slice(kh * group, (kh + 1) * group)
        q = all_q[:, span].reshape(total, HDIM)
        block = blk[:, :, kcols(kh)].reshape(sub_count * rows, HDIM)
        near = qkv[:, :, kcols(kh)].reshape(keys_q, HDIM)
        s0 = scores_of(q, block)
        s1 = jnp.where(
            seen, scores_of(q, near).reshape(shape4), masked_score
        ).reshape(total, keys_q)
        m = jnp.maximum(
            jnp.max(s0, axis=-1, keepdims=True), jnp.max(s1, axis=-1, keepdims=True)
        )
        acc = add_up(
            weights_of(s0, m), blk[:, :, vcols(kh)].reshape(sub_count * rows, HDIM)
        ) + add_up(weights_of(s1, m), qkv[:, :, vcols(kh)].reshape(keys_q, HDIM))
        sacc[:, span] = acc[:, :HDIM].astype(jnp.bfloat16).reshape(
            ctx_count, group, padded, HDIM
        )
        sums = acc[:, HDIM:]
        for z in range(ctx_count):
            for g in range(group):
                cut = slice((z * group + g) * padded, (z * group + g + 1) * padded)
                head = kh * group + g
                stats[z] = jnp.where(lane == head, m[cut], stats[z])
                stats[z] = jnp.where(lane == HDIM // 2 + head, sums[cut], stats[z])
        if kh == 0:
            point("near0")
    for z in range(ctx_count):
        sstat[z] = stats[z]

    def send_result(step, other, home):
        return pltpu.make_async_remote_copy(
            sacc.at[other], racc.at[home], r_send.at[other], r_recv.at[home],
            device_id={"ctx": other}, device_id_type=MESH,
        )

    def send_stat(step, other, home):
        return pltpu.make_async_remote_copy(
            sstat.at[other], rstat.at[home], t_send.at[other], t_recv.at[home],
            device_id={"ctx": other}, device_id_type=MESH,
        )

    for step in range(1, ctx_count):
        other = lax.rem(ctx + step, ctx_count)
        send_result(step, other, ctx).start()
        send_stat(step, other, ctx).start()
    racc[ctx] = sacc[ctx]
    rstat[ctx] = sstat[ctx]

    point("near1")

    def finish(kh, t, acc):
        done = (acc[:, :HDIM] / acc[:, HDIM:]).astype(jnp.bfloat16)
        start = pl.multiple_of(t * TILE, TILE)
        for g in range(group):
            head = kh * group + g
            out_ref[pl.ds(start, TILE), head * HDIM:(head + 1) * HDIM] = done[
                g * TILE:(g + 1) * TILE
            ]

    @pl.when(ctx == 0)
    def _():
        @pl.loop(0, tiles)
        def _(t):
            for kh in range(kv_heads):
                finish(kh, t, acc1[kh, t])

    @pl.when(ctx > 0)
    def _():
        for i in range(CHUNKS):
            recv_pair(i).wait_recv()

        @pl.loop(0, tiles)
        def _(t):
            for kh in range(kv_heads):
                _, acc = merged(
                    kh, t,
                    anc[:, :, :, kcols(kh)].reshape(sub_count * rows, HDIM),
                    anc[:, :, :, vcols(kh)].reshape(sub_count * rows, HDIM),
                )
                finish(kh, t, acc)

    for step in range(1, ctx_count):
        other = lax.rem(ctx + step, ctx_count)
        send_result(step, ctx, other).wait_recv()
        send_stat(step, ctx, other).wait_recv()

    got = [rstat[z] for z in range(ctx_count)]
    top = functools.reduce(jnp.maximum, got)
    scaled = [jnp.exp2((one - top) * exponent_scale) for one in got]
    for h in range(q_heads):
        above = jnp.zeros((padded, HDIM), jnp.float32)
        under = jnp.zeros((padded, 1), jnp.float32)
        for z in range(ctx_count):
            w = scaled[z][:, h:h + 1]
            above = above + w * racc[z, h].astype(jnp.float32)
            under = under + w * got[z][:, HDIM // 2 + h:HDIM // 2 + h + 1]
        qout_ref[:, h * HDIM:(h + 1) * HDIM] = (above / under).astype(jnp.bfloat16)

    swap(blk, blk_sem, sub).wait_send()
    swap(qkv, qkv_sem, sub).wait_send()
    for step in range(1, ctx_count):
        other = lax.rem(ctx + step, ctx_count)
        send_query(step).wait_send()
        send_result(step, other, ctx).wait_send()
        send_stat(step, other, ctx).wait_send()

    @pl.when(ctx == 0)
    def _():
        for i in range(CHUNKS):
            send_first(i).wait_send()

    @pl.when(ctx > 0)
    def _():
        for i in range(CHUNKS):
            send_pair(i).wait_send()

    @pl.when((ctx > 0) & (ctx < ctx_count - 1))
    def _():
        for i in range(CHUNKS):
            send_on(i).wait_send()


def turns(positions):
    half = HDIM // 2
    inverse = rope_base ** (-(jnp.arange(half, dtype=jnp.float32) * 2.0 / HDIM))
    angles = positions.astype(jnp.float32)[:, None] * inverse[None, :]
    cosine = jnp.cos(angles)
    sine = jnp.sin(angles)
    return cosine, sine


def shards(hidden, query_hidden, norm_gain, w_query, w_key, w_value):
    rows, width = hidden.shape
    query_rows = query_hidden.shape[0]
    padded = -(-query_rows // 16) * 16
    q_cols = w_query.shape[1]
    key_cols = w_key.shape[1]
    q_heads = q_cols // HDIM
    kv_heads = key_cols // HDIM
    group = q_heads // kv_heads
    tiles = rows // TILE
    ctx_count = lax.axis_size("ctx")
    sub_count = lax.axis_size("sub")
    ctx = lax.axis_index("ctx")
    sub = lax.axis_index("sub")
    if padded != query_rows:
        query_hidden = jnp.pad(query_hidden, ((0, padded - query_rows), (0, 0)))
    slot = ctx * sub_count + sub
    positions = jnp.concatenate(
        [
            slot * rows + jnp.arange(rows, dtype=jnp.int32),
            ctx_count * sub_count * rows
            + slot * query_rows
            + jnp.arange(padded, dtype=jnp.int32),
        ]
    )
    cosine, sine = turns(positions)
    wq_width = min(256, q_cols)
    bf16, f32 = jnp.bfloat16, jnp.float32
    dma = pltpu.SemaphoreType.DMA
    vmem = pl.BlockSpec(memory_space=pltpu.VMEM)
    hbm = pl.BlockSpec(memory_space=pl.ANY)
    out, qout = pl.pallas_call(
        functools.partial(kernel, (ctx_count, sub_count, query_rows)),
        out_shape=(
            pltpu.VMEM((rows, q_cols), bf16),
            pltpu.VMEM((padded, q_cols), bf16),
        ),
        in_specs=[hbm, hbm, vmem, vmem, vmem, hbm, hbm, hbm],
        out_specs=(vmem, vmem),
        scratch_shapes=[
            pltpu.VMEM((rows, width), bf16),
            pltpu.VMEM((padded, width), bf16),
            pltpu.VMEM((rows + padded, width), bf16),
            pltpu.VMEM((q_cols // wq_width, width, wq_width), bf16),
            pltpu.VMEM((width, key_cols), bf16),
            pltpu.VMEM((width, key_cols), bf16),
            pltpu.VMEM((q_heads, rows, HDIM), bf16),
            pltpu.VMEM((q_heads, padded, HDIM), bf16),
            pltpu.VMEM((ctx_count, q_heads, padded, HDIM), bf16),
            pltpu.VMEM((sub_count, rows, 2 * key_cols), bf16),
            pltpu.VMEM((sub_count, padded, 2 * key_cols), bf16),
            pltpu.VMEM((sub_count, CHUNKS, rows // CHUNKS, 2 * key_cols), bf16),
            pltpu.VMEM((kv_heads, tiles, group * TILE, 2 * HDIM), f32),
            pltpu.VMEM((kv_heads, tiles, group * TILE, HDIM), f32),
            pltpu.VMEM((ctx_count, q_heads, padded, HDIM), bf16),
            pltpu.VMEM((ctx_count, padded, HDIM), f32),
            pltpu.VMEM((ctx_count, q_heads, padded, HDIM), bf16),
            pltpu.VMEM((ctx_count, padded, HDIM), f32),
            pltpu.VMEM((rows + padded, HDIM), f32),
            pltpu.VMEM((rows + padded, HDIM), f32),
            dma((tiles,)), dma, dma, dma, dma((q_cols // wq_width,)),
            dma((2,)), dma((2,)),
            dma((CHUNKS,)), dma((CHUNKS,)), dma((CHUNKS,)), dma((CHUNKS,)),
            dma((ctx_count,)), dma((ctx_count,)), dma((ctx_count,)), dma((ctx_count,)),
            dma((ctx_count,)), dma((ctx_count,)),
        ],
        compiler_params=pltpu.CompilerParams(
            collective_id=0, has_side_effects=True, vmem_limit_bytes=58 * 1024 * 1024
        ),
    )(hidden, query_hidden, norm_gain.reshape(1, width), cosine, sine, w_query, w_key, w_value)
    return out, qout[:query_rows]


def solution(mesh):
    return jax.shard_map(
        shards,
        mesh=mesh,
        in_specs=(
            P(("grp", "ctx", "sub"), None),
            P(("grp", "ctx", "sub"), None),
            P(),
            P(None, "head"),
            P(None, "head"),
            P(None, "head"),
        ),
        out_specs=(P(("grp", "ctx", "sub"), "head"), P(("grp", "ctx", "sub"), "head")),
        check_vma=False,
    )
```

```python
import functools
import math

import jax
import jax.numpy as jnp
from jax import lax
from jax.experimental import pallas as pl
from jax.experimental.pallas import tpu as pltpu
from jax.sharding import PartitionSpec as P

HDIM = 128
TILE = 128
CHUNKS = 8

LATEST = 3
SCHEDULE = {
    1: ["q1", "q1", "q2", "q2", "q3", "q3", "d1", "d3"],
    2: ["q3", "q3", "d1", "d2", "d3", "d3", "peer", "peer"],
    LATEST: ["peer", "peer", "near0", "near0", "half", "half", "half", "half"],
}

rope_base = 500000.0
norm_eps = 1e-05
masked_score = -1e30
exponent_scale = HDIM ** (-0.5) * math.log2(math.e)

MESH = pl.DeviceIdType.MESH
NT_DIMS = (((1,), (1,)), ((), ()))


def kernel(
    sizes,
    hidden_hbm, qhidden_hbm, gain_ref, cosine_ref, sine_ref, wq_hbm, wk_hbm, wv_hbm,
    out_ref, qout_ref,
    hid, qhid, normed, wq, wk, wv, heads_q, own_q, all_q, blk, qkv, anc,
    acc1, max1, sacc, sstat, racc, rstat, cos_ref, sin_ref,
    load_sem, qload_sem, wk_sem, wv_sem, wq_sem,
    blk_sem, qkv_sem, chain_send, chain_recv, pair_send, pair_recv,
    q_send, q_recv, r_send, r_recv, t_send, t_recv,
):
    ctx_count, sub_count, query_rows = sizes
    rows, width = hid.shape
    padded = qhid.shape[0]
    q_heads = heads_q.shape[0]
    key_cols = wk.shape[1]
    kv_heads = key_cols // HDIM
    group = q_heads // kv_heads
    tiles = rows // TILE
    part = rows // CHUNKS
    ctx = lax.axis_index("ctx")
    sub = lax.axis_index("sub")
    peer = lax.rem(sub + 1, sub_count)

    def load_rows(i):
        piece = pl.ds(i * TILE, TILE)
        return pltpu.make_async_copy(hidden_hbm.at[piece], hid.at[piece], load_sem.at[i])

    wq_width = wq.shape[2]
    wq_tiles = wq.shape[0]

    def load_wq(j):
        return pltpu.make_async_copy(
            wq_hbm.at[:, pl.ds(j * wq_width, wq_width)], wq.at[j], wq_sem.at[j]
        )

    load_query = pltpu.make_async_copy(qhidden_hbm, qhid, qload_sem)
    load_wk = pltpu.make_async_copy(wk_hbm, wk, wk_sem)
    load_wv = pltpu.make_async_copy(wv_hbm, wv, wv_sem)
    for i in range(tiles):
        load_rows(i).start()
    load_query.start()
    load_wk.start()
    load_wv.start()
    for j in range(wq_tiles):
        load_wq(j).start()

    barrier = pltpu.get_barrier_semaphore()
    for step in range(1, ctx_count):
        other = lax.rem(ctx + step, ctx_count)
        pl.semaphore_signal(barrier, inc=1, device_id={"ctx": other}, device_id_type=MESH)
    pl.semaphore_signal(barrier, inc=1, device_id={"sub": peer}, device_id_type=MESH)

    cos_ref[...] = jnp.concatenate([cosine_ref[...], cosine_ref[...]], axis=1)
    sin_ref[...] = jnp.concatenate([-sine_ref[...], sine_ref[...]], axis=1)
    gain = gain_ref[...]

    def norm_rows(source, start, target, count):
        wide = source[pl.ds(start, count), :].astype(jnp.float32)
        meansq = jnp.mean(wide * wide, axis=-1, keepdims=True) + norm_eps
        wide = source[pl.ds(start, count), :].astype(jnp.float32)
        normed[pl.ds(target, count), :] = (wide * lax.rsqrt(meansq) * gain).astype(jnp.bfloat16)

    for i in range(tiles):
        load_rows(i).wait()

        @pl.loop(0, TILE // 16, unroll=2)
        def _(b):
            start = pl.multiple_of(i * TILE + b * 16, 16)
            norm_rows(hid, start, start, 16)

    load_query.wait()
    for b in range(padded // 16):
        norm_rows(qhid, b * 16, rows + b * 16, 16)

    def rotated(values, head):
        cols = values[:, head * HDIM:(head + 1) * HDIM]
        return (cols * cos_ref[...] + pltpu.roll(cols, HDIM // 2, 1) * sin_ref[...]).astype(
            jnp.bfloat16
        )

    load_wk.wait()
    keys = jnp.dot(normed[...], wk[...], preferred_element_type=jnp.float32)
    for h in range(kv_heads):
        turned = rotated(keys, h)
        blk[sub, :, pl.ds(h * HDIM, HDIM)] = turned[:rows]
        qkv[sub, :, pl.ds(h * HDIM, HDIM)] = turned[rows:]
    load_wv.wait()
    values = jnp.dot(normed[...], wv[...], preferred_element_type=jnp.float32).astype(jnp.bfloat16)
    blk[sub, :, pl.ds(key_cols, key_cols)] = values[:rows]
    qkv[sub, :, pl.ds(key_cols, key_cols)] = values[rows:]

    pl.semaphore_wait(barrier, ctx_count)

    below = lax.rem(ctx + 1, ctx_count)

    def send_first(i):
        return pltpu.make_async_remote_copy(
            blk.at[sub, pl.ds(i * part, part)], anc.at[sub, i],
            chain_send.at[i], chain_recv.at[i],
            device_id={"ctx": below}, device_id_type=MESH,
        )

    def send_on(i):
        return pltpu.make_async_remote_copy(
            anc.at[sub, i], anc.at[sub, i],
            chain_send.at[i], chain_recv.at[i],
            device_id={"ctx": below}, device_id_type=MESH,
        )

    def send_pair(i):
        return pltpu.make_async_remote_copy(
            anc.at[sub, i], anc.at[sub, i],
            pair_send.at[i], pair_recv.at[i],
            device_id={"sub": peer}, device_id_type=MESH,
        )

    def recv_pair(i):
        return pltpu.make_async_remote_copy(
            anc.at[peer, i], anc.at[peer, i],
            pair_send.at[i], pair_recv.at[i],
            device_id={"sub": peer}, device_id_type=MESH,
        )

    @pl.when(ctx == 0)
    def _():
        for i in range(CHUNKS):
            send_first(i).start()

    def swap(ref, sems, place):
        return pltpu.make_async_remote_copy(
            ref.at[place], ref.at[place], sems.at[0], sems.at[1],
            device_id={"sub": peer}, device_id_type=MESH,
        )

    swap(blk, blk_sem, sub).start()
    swap(qkv, qkv_sem, sub).start()

    def forward(i):
        send_on(i).wait_recv()

        @pl.when(ctx < ctx_count - 1)
        def _():
            send_on(i).start()

        send_pair(i).start()

    def point(name):
        for place, plan in SCHEDULE.items():
            due = [i for i in range(CHUNKS) if plan[i] == name]
            if due:
                @pl.when(ctx >= place if place == LATEST else ctx == place)
                def _():
                    for i in due:
                        forward(i)

    per_tile = wq_width // HDIM
    for j in range(wq_tiles):
        load_wq(j).wait()

        made = jnp.dot(normed[...], wq[j], preferred_element_type=jnp.float32)
        for t in range(per_tile):
            turned = rotated(made, t)
            heads_q[j * per_tile + t] = turned[:rows]
            own_q[j * per_tile + t] = turned[rows:]
        for at in range(3):
            if at * wq_tiles // 4 == j:
                point(f"q{at}")

    def send_query(step):
        other = lax.rem(ctx + step, ctx_count)
        return pltpu.make_async_remote_copy(
            own_q, all_q.at[ctx], q_send.at[other], q_recv.at[ctx],
            device_id={"ctx": other}, device_id_type=MESH,
        )

    def recv_query(step):
        other = lax.rem(ctx + step, ctx_count)
        return pltpu.make_async_remote_copy(
            own_q, all_q.at[other], q_send.at[other], q_recv.at[other],
            device_id={"ctx": other}, device_id_type=MESH,
        )

    for step in range(1, ctx_count):
        send_query(step).start()
    all_q[ctx] = own_q[...]

    point("q3")

    def scores_of(q, k):
        return lax.dot_general(q, k, NT_DIMS, preferred_element_type=jnp.float32)

    def weights_of(s, m):
        return jnp.exp2((s - m) * exponent_scale).astype(jnp.bfloat16)

    def with_ones(v):
        return jnp.concatenate([v, jnp.ones_like(v)], axis=1)

    def add_up(p, v):
        return jnp.dot(p, with_ones(v), preferred_element_type=jnp.float32)

    def kcols(kh):
        return slice(kh * HDIM, (kh + 1) * HDIM)

    def vcols(kh):
        return slice(key_cols + kh * HDIM, key_cols + (kh + 1) * HDIM)

    def tile_q(kh, start):
        return heads_q[kh * group:(kh + 1) * group, pl.ds(start, TILE), :].reshape(
            group * TILE, HDIM
        )

    for t in range(tiles):
        span = (t + 1) * TILE
        for kh in range(kv_heads):
            s = scores_of(tile_q(kh, t * TILE), blk[sub, :span, kcols(kh)])
            row = lax.broadcasted_iota(jnp.int32, (TILE, span), 0) + t * TILE
            col = lax.broadcasted_iota(jnp.int32, (TILE, span), 1)
            s = jnp.where(
                (row >= col)[None], s.reshape(group, TILE, span), masked_score
            ).reshape(group * TILE, span)
            m = jnp.max(s, axis=-1, keepdims=True)
            acc1[kh, t] = add_up(weights_of(s, m), blk[sub, :span, vcols(kh)])
            max1[kh, t] = jnp.broadcast_to(m, (group * TILE, HDIM))
        for at in range(4):
            if at * tiles // 4 == t:
                point(f"d{at}")

    def merged(kh, t, k, v):
        s = scores_of(tile_q(kh, pl.multiple_of(t * TILE, TILE)), k)
        before = max1[kh, t]
        m = jnp.maximum(jnp.max(s, axis=-1, keepdims=True), before)
        factor = jnp.exp2((before - m) * exponent_scale)
        acc = acc1[kh, t] * jnp.concatenate([factor, factor], axis=1)
        return m, acc + add_up(weights_of(s, m[:, :1]), v)

    swap(blk, blk_sem, peer).wait_recv()
    swap(qkv, qkv_sem, peer).wait_recv()

    @pl.when(sub > 0)
    def _():
        @pl.loop(0, tiles)
        def _(t):
            for kh in range(kv_heads):
                m, acc = merged(kh, t, blk[0, :, kcols(kh)], blk[0, :, vcols(kh)])
                acc1[kh, t] = acc
                max1[kh, t] = m

    point("peer")

    for step in range(1, ctx_count):
        recv_query(step).wait_recv()

    total = ctx_count * group * padded
    keys_q = sub_count * padded
    shape4 = (ctx_count, group, padded, keys_q)
    owner = lax.broadcasted_iota(jnp.int32, shape4, 0)
    place = lax.broadcasted_iota(jnp.int32, shape4, 2)
    key_at = lax.broadcasted_iota(jnp.int32, shape4, 3)
    query_pos = (owner * sub_count + sub) * query_rows + place
    key_sub = jnp.where(key_at >= padded, 1, 0)
    key_row = key_at - key_sub * padded
    key_pos = (ctx * sub_count + key_sub) * query_rows + key_row
    seen = (query_pos >= key_pos) & (key_row < query_rows)
    lane = lax.broadcasted_iota(jnp.int32, (padded, HDIM), 1)
    stats = [jnp.zeros((padded, HDIM), jnp.float32) for _ in range(ctx_count)]
    for kh in range(kv_heads):
        span = slice(kh * group, (kh + 1) * group)
        q = all_q[:, span].reshape(total, HDIM)
        block = blk[:, :, kcols(kh)].reshape(sub_count * rows, HDIM)
        near = qkv[:, :, kcols(kh)].reshape(keys_q, HDIM)
        s0 = scores_of(q, block)
        s1 = jnp.where(
            seen, scores_of(q, near).reshape(shape4), masked_score
        ).reshape(total, keys_q)
        m = jnp.maximum(
            jnp.max(s0, axis=-1, keepdims=True), jnp.max(s1, axis=-1, keepdims=True)
        )
        acc = add_up(
            weights_of(s0, m), blk[:, :, vcols(kh)].reshape(sub_count * rows, HDIM)
        ) + add_up(weights_of(s1, m), qkv[:, :, vcols(kh)].reshape(keys_q, HDIM))
        sacc[:, span] = acc[:, :HDIM].astype(jnp.bfloat16).reshape(
            ctx_count, group, padded, HDIM
        )
        sums = acc[:, HDIM:]
        for z in range(ctx_count):
            for g in range(group):
                cut = slice((z * group + g) * padded, (z * group + g + 1) * padded)
                head = kh * group + g
                stats[z] = jnp.where(lane == head, m[cut], stats[z])
                stats[z] = jnp.where(lane == HDIM // 2 + head, sums[cut], stats[z])
        if kh == 0:
            point("near0")
    for z in range(ctx_count):
        sstat[z] = stats[z]

    def send_result(step, other, home):
        return pltpu.make_async_remote_copy(
            sacc.at[other], racc.at[home], r_send.at[other], r_recv.at[home],
            device_id={"ctx": other}, device_id_type=MESH,
        )

    def send_stat(step, other, home):
        return pltpu.make_async_remote_copy(
            sstat.at[other], rstat.at[home], t_send.at[other], t_recv.at[home],
            device_id={"ctx": other}, device_id_type=MESH,
        )

    for step in range(1, ctx_count):
        other = lax.rem(ctx + step, ctx_count)
        send_result(step, other, ctx).start()
        send_stat(step, other, ctx).start()
    racc[ctx] = sacc[ctx]
    rstat[ctx] = sstat[ctx]

    point("near1")

    def finish(kh, t, acc):
        done = (acc[:, :HDIM] / acc[:, HDIM:]).astype(jnp.bfloat16)
        start = pl.multiple_of(t * TILE, TILE)
        for g in range(group):
            head = kh * group + g
            out_ref[pl.ds(start, TILE), head * HDIM:(head + 1) * HDIM] = done[
                g * TILE:(g + 1) * TILE
            ]

    @pl.when(ctx == 0)
    def _():
        @pl.loop(0, tiles)
        def _(t):
            for kh in range(kv_heads):
                finish(kh, t, acc1[kh, t])

    @pl.when(ctx > 0)
    def _():
        half = CHUNKS // 2

        def anchor_part(first, kh, t):
            keys_in = sub_count * half * part
            return merged(
                kh, t,
                anc[:, first:first + half, :, kcols(kh)].reshape(keys_in, HDIM),
                anc[:, first:first + half, :, vcols(kh)].reshape(keys_in, HDIM),
            )

        for i in range(half):
            recv_pair(i).wait_recv()

        @pl.loop(0, tiles)
        def _(t):
            for kh in range(kv_heads):
                m, acc = anchor_part(0, kh, t)
                acc1[kh, t] = acc
                max1[kh, t] = m

        point("half")
        for i in range(half, CHUNKS):
            recv_pair(i).wait_recv()

        @pl.loop(0, tiles)
        def _(t):
            for kh in range(kv_heads):
                _, acc = anchor_part(half, kh, t)
                finish(kh, t, acc)

    for step in range(1, ctx_count):
        other = lax.rem(ctx + step, ctx_count)
        send_result(step, ctx, other).wait_recv()
        send_stat(step, ctx, other).wait_recv()

    got = [rstat[z] for z in range(ctx_count)]
    top = functools.reduce(jnp.maximum, got)
    scaled = [jnp.exp2((one - top) * exponent_scale) for one in got]
    for h in range(q_heads):
        above = jnp.zeros((padded, HDIM), jnp.float32)
        under = jnp.zeros((padded, 1), jnp.float32)
        for z in range(ctx_count):
            w = scaled[z][:, h:h + 1]
            above = above + w * racc[z, h].astype(jnp.float32)
            under = under + w * got[z][:, HDIM // 2 + h:HDIM // 2 + h + 1]
        qout_ref[:, h * HDIM:(h + 1) * HDIM] = (above / under).astype(jnp.bfloat16)

    swap(blk, blk_sem, sub).wait_send()
    swap(qkv, qkv_sem, sub).wait_send()
    for step in range(1, ctx_count):
        other = lax.rem(ctx + step, ctx_count)
        send_query(step).wait_send()
        send_result(step, other, ctx).wait_send()
        send_stat(step, other, ctx).wait_send()

    @pl.when(ctx == 0)
    def _():
        for i in range(CHUNKS):
            send_first(i).wait_send()

    @pl.when(ctx > 0)
    def _():
        for i in range(CHUNKS):
            send_pair(i).wait_send()

    @pl.when((ctx > 0) & (ctx < ctx_count - 1))
    def _():
        for i in range(CHUNKS):
            send_on(i).wait_send()


def turns(positions):
    half = HDIM // 2
    inverse = rope_base ** (-(jnp.arange(half, dtype=jnp.float32) * 2.0 / HDIM))
    angles = positions.astype(jnp.float32)[:, None] * inverse[None, :]
    cosine = jnp.cos(angles)
    sine = jnp.sin(angles)
    return cosine, sine


def shards(hidden, query_hidden, norm_gain, w_query, w_key, w_value):
    rows, width = hidden.shape
    query_rows = query_hidden.shape[0]
    padded = -(-query_rows // 16) * 16
    q_cols = w_query.shape[1]
    key_cols = w_key.shape[1]
    q_heads = q_cols // HDIM
    kv_heads = key_cols // HDIM
    group = q_heads // kv_heads
    tiles = rows // TILE
    ctx_count = lax.axis_size("ctx")
    sub_count = lax.axis_size("sub")
    ctx = lax.axis_index("ctx")
    sub = lax.axis_index("sub")
    if padded != query_rows:
        query_hidden = jnp.pad(query_hidden, ((0, padded - query_rows), (0, 0)))
    slot = ctx * sub_count + sub
    positions = jnp.concatenate(
        [
            slot * rows + jnp.arange(rows, dtype=jnp.int32),
            ctx_count * sub_count * rows
            + slot * query_rows
            + jnp.arange(padded, dtype=jnp.int32),
        ]
    )
    cosine, sine = turns(positions)
    wq_width = min(256, q_cols)
    bf16, f32 = jnp.bfloat16, jnp.float32
    dma = pltpu.SemaphoreType.DMA
    vmem = pl.BlockSpec(memory_space=pltpu.VMEM)
    hbm = pl.BlockSpec(memory_space=pl.ANY)
    out, qout = pl.pallas_call(
        functools.partial(kernel, (ctx_count, sub_count, query_rows)),
        out_shape=(
            pltpu.VMEM((rows, q_cols), bf16),
            pltpu.VMEM((padded, q_cols), bf16),
        ),
        in_specs=[hbm, hbm, vmem, vmem, vmem, hbm, hbm, hbm],
        out_specs=(vmem, vmem),
        scratch_shapes=[
            pltpu.VMEM((rows, width), bf16),
            pltpu.VMEM((padded, width), bf16),
            pltpu.VMEM((rows + padded, width), bf16),
            pltpu.VMEM((q_cols // wq_width, width, wq_width), bf16),
            pltpu.VMEM((width, key_cols), bf16),
            pltpu.VMEM((width, key_cols), bf16),
            pltpu.VMEM((q_heads, rows, HDIM), bf16),
            pltpu.VMEM((q_heads, padded, HDIM), bf16),
            pltpu.VMEM((ctx_count, q_heads, padded, HDIM), bf16),
            pltpu.VMEM((sub_count, rows, 2 * key_cols), bf16),
            pltpu.VMEM((sub_count, padded, 2 * key_cols), bf16),
            pltpu.VMEM((sub_count, CHUNKS, rows // CHUNKS, 2 * key_cols), bf16),
            pltpu.VMEM((kv_heads, tiles, group * TILE, 2 * HDIM), f32),
            pltpu.VMEM((kv_heads, tiles, group * TILE, HDIM), f32),
            pltpu.VMEM((ctx_count, q_heads, padded, HDIM), bf16),
            pltpu.VMEM((ctx_count, padded, HDIM), f32),
            pltpu.VMEM((ctx_count, q_heads, padded, HDIM), bf16),
            pltpu.VMEM((ctx_count, padded, HDIM), f32),
            pltpu.VMEM((rows + padded, HDIM), f32),
            pltpu.VMEM((rows + padded, HDIM), f32),
            dma((tiles,)), dma, dma, dma, dma((q_cols // wq_width,)),
            dma((2,)), dma((2,)),
            dma((CHUNKS,)), dma((CHUNKS,)), dma((CHUNKS,)), dma((CHUNKS,)),
            dma((ctx_count,)), dma((ctx_count,)), dma((ctx_count,)), dma((ctx_count,)),
            dma((ctx_count,)), dma((ctx_count,)),
        ],
        compiler_params=pltpu.CompilerParams(
            collective_id=0, has_side_effects=True, vmem_limit_bytes=58 * 1024 * 1024
        ),
    )(hidden, query_hidden, norm_gain.reshape(1, width), cosine, sine, w_query, w_key, w_value)
    return out, qout[:query_rows]


def solution(mesh):
    return jax.shard_map(
        shards,
        mesh=mesh,
        in_specs=(
            P(("grp", "ctx", "sub"), None),
            P(("grp", "ctx", "sub"), None),
            P(),
            P(None, "head"),
            P(None, "head"),
            P(None, "head"),
        ),
        out_specs=(P(("grp", "ctx", "sub"), "head"), P(("grp", "ctx", "sub"), "head")),
        check_vma=False,
    )
```
